512 devices in a mesh: chan: 64 (over z, y), blk: 8 (over x, core).
Axes of the slice: x: 4, y: 4, z: 16, core: 2. Of those that a mesh axis runs over, the one named last changes fastest.
Arguments:
- amps_pp: bfloat16 [64, 3584, 512], P('chan', 'blk'), may hold values from -6 to 6
- source_pp: bfloat16 [64, 3584, 512], P('chan', 'blk'), may hold values from -6 to 6
- cycle_interaction: bfloat16 [64, 3584, 3584], P('chan', 'blk'), may hold values from -1 to 1, as said below
- to_ph_rows: int32 [64, 3584, 2], P('chan', 'blk'), may hold values from 0 to 447
- to_ph_coef: int32 [64, 3584, 2], P('chan', 'blk'), may hold values from 0 to 255
- to_pp_rows: int32 [64, 3584, 2], P('chan', 'blk'), may hold values from 0 to 447
- to_pp_coef: int32 [64, 3584, 2], P('chan', 'blk'), may hold values from 0 to 255
- sixj: bfloat16 [256], replicated, may hold values from -1 to 1
- pp_sizes: int32 [64], replicated, may hold values from 1 to 3584, 76458 in all
- ph_sizes: int32 [64], replicated, may hold values from 1 to 3584, 76458 in all
- particle_energy: float32 [64, 3584], P('chan', 'blk'), may hold values from 1 to 4
- hole_energy: float32 [64, 512], P('chan'), may hold values from -3 to -0.5
Outputs:
- new_amps: bfloat16 [64, 3584, 512], P('chan', 'blk')
The draws below stay inside these ranges and needn't reach their ends.
Inputs may be any that keep to these rules, and one draw needn't show every extreme that they name: `to_ph_rows`: row numbers within one device's block of 448 rows. `to_pp_rows`: row numbers within one device's block of 448 rows. `cycle_interaction`: each channel's matrix is symmetric.
All inputs are finite; a program needn't handle non-finite values.
Results may differ from the reference program's by a relative error of at most 0.0095.
Values may be sent and summed in bfloat16 or wider, within the bound.
A program may use at most 64 MiB of HBM per device.

```python
import math
import jax
import jax.numpy as jnp
import numpy as np
from jax import lax

HH = 512
CAP = 3584
NSIX = 256
CHANNELS = 64
ROWS_DEV = 448
SLOT = 7
N_BLK = 8


def draw_cycle_interaction(key, part):
    key = jax.random.fold_in(key, 7)
    keys = jax.random.split(key, CHANNELS)

    def one(single):
        base = jax.random.normal(single, (CAP, CAP), jnp.float32)
        sym = (base + base.T) * 0.5 ** 0.5 * CAP ** (-0.5)
        return sym.astype(jnp.bfloat16)
    return lax.map(one, keys)


def with_ends(values, rng, low, largest):
    longest = values.shape.index(max(values.shape))
    spots = []
    for shift in (0, 1):
        where = [jax.random.randint(jax.random.fold_in(rng, axis), (), 0, length) for axis, length in enumerate(values.shape)]
        where[longest] = (where[longest] + shift) % values.shape[longest]
        spots.append(tuple(where))
    return values.at[spots[0]].set(low).at[spots[1]].set(largest)


def block_levels(stream_key, dims, shards, least, high):
    level = 1.0
    for dim, parts in shards:
        heights = jax.random.uniform(jax.random.fold_in(jax.random.fold_in(stream_key, 6), dim), (parts,), jnp.float32, least / len(shards), high / len(shards))
        level = level * jnp.repeat(jnp.exp(heights), dims[dim] // parts).reshape((-1,) + (1,) * (len(dims) - 1 - dim))
    return level


def profile(amount, total, most, skew):
    portions = [(1 << 20) // math.isqrt(standing ** skew) + 1 for standing in range(2, amount + 1)]
    surplus, holding = total - most - (amount - 1), [1] * (amount - 1)
    while surplus > 0:
        movable = [i for i in range(amount - 1) if holding[i] < most]
        pool, budget = sum([portions[i] for i in movable]), surplus
        for i in movable:
            extra = min(most - holding[i], max(1, budget * portions[i] // pool), surplus)
            holding[i] = holding[i] + extra
            surplus = surplus - extra
    return np.array([most] + holding)


def uneven_parts(stream_key, count, total, most, slope):
    if count == 2:
        one = jax.random.randint(stream_key, (), max(1, total - most), min(most, total - 1) + 1)
        return jnp.stack([one, total - one])
    sizes = jnp.asarray(profile(count, total, most, slope), jnp.int32)
    pairs = (count - 1) // 2
    giver, sink = sizes[1:1 + 2 * pairs:2], sizes[2:2 + 2 * pairs:2]
    room = jnp.minimum(giver - 1, most - sink)
    shifted = jax.random.randint(jax.random.fold_in(stream_key, 1), (pairs,), 0, 1 << 20) % (room + 1)
    sizes = sizes.at[1:1 + 2 * pairs:2].set(giver - shifted).at[2:2 + 2 * pairs:2].set(sink + shifted)
    return sizes[jax.random.permutation(jax.random.fold_in(stream_key, 2), count)]


def gaussian(key, shape, spread, limit, cuts=(), held_as=jnp.bfloat16):
    gain = block_levels(key, shape, cuts, -0.22, 0.18) if cuts else 1.0
    drawn = jax.random.normal(key, shape, jnp.float32) * spread * gain
    return jnp.minimum(jnp.maximum(drawn, -limit), limit).astype(held_as)


def setup_inputs(seed: int = 0) -> dict:
    key_of = jax.random.split(jax.random.key(seed), 13)
    return {
        "amps_pp": gaussian(key_of[0], (CHANNELS, CAP, HH), 1.0, 6.0, ((0, 64), (1, 8))),
        "source_pp": gaussian(key_of[1], (CHANNELS, CAP, HH), 1.0, 6.0, ((0, 64), (1, 8))),
        "cycle_interaction": draw_cycle_interaction(jax.random.fold_in(key_of[12], 71), 0),
        "to_ph_rows": with_ends(jax.random.randint(key_of[3], (CHANNELS, CAP, 2), 0, ROWS_DEV), jax.random.fold_in(key_of[3], 1), 0, ROWS_DEV - 1).astype(jnp.int32),
        "to_ph_coef": with_ends(jax.random.randint(key_of[4], (CHANNELS, CAP, 2), 0, NSIX), jax.random.fold_in(key_of[4], 1), 0, NSIX - 1).astype(jnp.int32),
        "to_pp_rows": with_ends(jax.random.randint(key_of[5], (CHANNELS, CAP, 2), 0, ROWS_DEV), jax.random.fold_in(key_of[5], 1), 0, ROWS_DEV - 1).astype(jnp.int32),
        "to_pp_coef": with_ends(jax.random.randint(key_of[6], (CHANNELS, CAP, 2), 0, NSIX), jax.random.fold_in(key_of[6], 1), 0, NSIX - 1).astype(jnp.int32),
        "sixj": jnp.clip(jax.random.uniform(key_of[7], (NSIX,), jnp.float32, -1.0, 1.0), -1.0, 1.0).astype(jnp.bfloat16),
        "pp_sizes": uneven_parts(key_of[8], CHANNELS, CAP * CHANNELS // 3, CAP, 2).astype(jnp.int32),
        "ph_sizes": uneven_parts(key_of[9], CHANNELS, CAP * CHANNELS // 3, CAP, 2).astype(jnp.int32),
        "particle_energy": jnp.clip(jnp.exp(math.log(4.0) - 1.3862944 * jax.random.uniform(key_of[10], (CHANNELS, CAP), jnp.float32) ** block_levels(key_of[10], (CHANNELS, CAP), ((0, 64), (1, 8)), -0.2, 0.2)), 1.0, 4.0),
        "hole_energy": jnp.clip(-3.0 + 2.5 * jax.random.uniform(key_of[11], (CHANNELS, HH), jnp.float32) ** block_levels(key_of[11], (CHANNELS, HH), ((0, 64),), -0.2, 0.2), -3.0, -0.5),
    }


def recouple(rows, index, table, sixj):
    coef = sixj.astype(jnp.float32)[table]

    def one(args):
        block, where, weight = args
        blocked = block.reshape(N_BLK, ROWS_DEV, HH).astype(jnp.float32)
        where = where.reshape(N_BLK, ROWS_DEV, 2)
        weight = weight.reshape(N_BLK, ROWS_DEV, 2)
        first = jax.vmap(lambda a, b: jnp.take(a, b, axis=0))(blocked, where[:, :, 0])
        second = jax.vmap(lambda a, b: jnp.take(a, b, axis=0))(blocked, where[:, :, 1])
        slots = first * weight[:, :, 0:1] + second * weight[:, :, 1:2]
        return slots.astype(jnp.bfloat16)

    slots = lax.map(one, (rows, index, coef))
    slots = slots.reshape(CHANNELS, N_BLK, CHANNELS, SLOT, HH).transpose(2, 1, 0, 3, 4)
    return slots.reshape(CHANNELS, CAP, HH)


def cycle_one(args):
    inter, amps = args
    columns = inter.reshape(CAP, N_BLK, ROWS_DEV).astype(jnp.float32)
    pieces = amps.reshape(N_BLK, ROWS_DEV, HH).astype(jnp.float32)
    terms = jnp.einsum("cbr,brh->bch", columns, pieces)
    terms = lax.optimization_barrier(terms.astype(jnp.bfloat16)).astype(jnp.float32)
    return jnp.sum(terms, axis=0)


def reference(amps_pp, source_pp, cycle_interaction, to_ph_rows, to_ph_coef, to_pp_rows, to_pp_coef, sixj, pp_sizes, ph_sizes, particle_energy, hole_energy):
    row_ids = jnp.arange(CAP, dtype=jnp.int32)
    amps_ph = recouple(amps_pp, to_ph_rows, to_ph_coef, sixj)
    live_ph = row_ids[None, :] < ph_sizes[:, None]
    amps_ph = jnp.where(live_ph[:, :, None], amps_ph, jnp.zeros_like(amps_ph))
    cycle = lax.map(cycle_one, (cycle_interaction, amps_ph))
    back = recouple(cycle, to_pp_rows, to_pp_coef, sixj)
    denom = particle_energy[:, :, None] - hole_energy[:, None, :]
    value = (source_pp.astype(jnp.float32) + back.astype(jnp.float32)) / denom
    live_pp = row_ids[None, :] < pp_sizes[:, None]
    value = jnp.where(live_pp[:, :, None], value, jnp.zeros_like(value))
    return value.astype(jnp.bfloat16)
```

```python
import functools

import jax
import jax.numpy as jnp
from jax import lax
from jax.experimental import pallas as pl
from jax.experimental.pallas import tpu as pltpu
from jax.sharding import PartitionSpec as P

MESH = pl.DeviceIdType.MESH
BF = jnp.bfloat16
F32 = jnp.float32
I32 = jnp.int32
NZ, NY, NX = 16, 4, 4
SLOT = 7
U = NY * SLOT
ROWS = NZ * U
STACK = 4 * U
FWD = (0, 32, 64, 96, 112)
BWD = (0, 16, 48, 80, 112)
WIN = ((0, 32), (16, 64), (48, 96), (80, 112))


def iota(shape, dim):
    return lax.broadcasted_iota(I32, shape, dim)


def div7(v):
    return (v * 9363) >> 16


def div28(v):
    return (v * 2341) >> 16


def div112(v):
    return (v * 586) >> 16


def onehot_rows(column, width):
    hit = iota((column.shape[0], width), 1) == column
    return jnp.where(hit, 1.0, 0.0).astype(BF)


def natural_of(p):
    y = div112(p)
    r = p - y * 112
    z = div7(r)
    return (z * NY + y) * SLOT + (r - z * SLOT)


def dot(a, b):
    return jnp.dot(a, b, preferred_element_type=F32)


def dot_tn(a, b):
    return lax.dot_general(a, b, (((0,), (0,)), ((), ())), preferred_element_type=F32)


def weights(rows_ref, coef_ref, sixj, k, live):
    picked = (iota((256, ROWS), 0) == coef_ref[k : k + 1, :]).astype(F32).astype(BF)
    c = dot(sixj, picked)[0:1, :]
    if live is not None:
        c = jnp.where(live, c, 0.0)
    return jnp.where(iota((ROWS, ROWS), 0) == rows_ref[k : k + 1, :], c, 0.0)


def kernel(
    amps_ref,
    phr_ref,
    phc_ref,
    ppr_ref,
    ppc_ref,
    sixj_ref,
    pps_ref,
    phs_ref,
    pe_ref,
    he_ref,
    inter_hbm,
    src_hbm,
    out_ref,
    inter,
    src,
    ip,
    sf,
    rf,
    sy,
    g,
    ts,
    ry,
    sb,
    rb,
    mid0,
    mid1,
    mid2,
    mid3,
    back0,
    back1,
    back2,
    back3,
    fin0,
    fin1,
    fin2,
    fin3,
    pcol,
    load_sem,
    fs,
    fr,
    gs,
    gr,
    cs,
    cr,
    ys,
    yr,
    bs,
    br,
):
    chan = lax.axis_index("chan")
    blk = lax.axis_index("blk")
    z = chan // NY
    y = lax.rem(chan, NY)
    x = blk // 2
    core = lax.rem(blk, 2)
    other = 1 - core
    mid = (mid0, mid1, mid2, mid3)
    backs = (back0, back1, back2, back3)
    fin = (fin0, fin1, fin2, fin3)

    def z_target(i):
        j = 15 - i - 1
        m = j // 2 + 1
        d = m + lax.rem(j, 2) * (NZ - 2 * m)
        return lax.rem(z + d, NZ)

    def yx_target(i):
        return lax.rem(y + lax.rem(i, NY), NY), lax.rem(x + i // NY, NX)

    barrier = pltpu.get_barrier_semaphore()

    def greet_z(i, _):
        pl.semaphore_signal(
            barrier, inc=1, device_id=(z_target(i) * NY + y, blk), device_id_type=MESH
        )
        return 0

    def greet_yx(i, _):
        ty, tx = yx_target(i)
        pl.semaphore_signal(
            barrier, inc=1, device_id=(z * NY + ty, tx * 2 + core), device_id_type=MESH
        )
        return 0

    lax.fori_loop(0, 15, greet_z, 0)
    lax.fori_loop(1, 16, greet_yx, 0)
    pl.semaphore_signal(barrier, inc=1, device_id=(chan, x * 2 + other), device_id_type=MESH)

    load_inter = pltpu.make_async_copy(inter_hbm, inter, load_sem.at[0])
    load_src = pltpu.make_async_copy(src_hbm, src, load_sem.at[1])
    load_inter.start()
    load_src.start()

    sixj = jnp.broadcast_to(sixj_ref[...].astype(F32), (16, 256)).astype(BF)
    s16 = iota((16, 64), 0)
    sizes = phs_ref[...]
    parts = jnp.where(
        s16 == 0,
        sizes >> 6,
        jnp.where(s16 == 1, sizes & 63, jnp.where(s16 == 2, iota((16, 64), 1), 0)),
    )
    owner = div7(iota((64, ROWS), 1)) == iota((64, ROWS), 0)
    spread = dot(parts.astype(F32).astype(BF), jnp.where(owner, 1.0, 0.0).astype(BF))
    limit = spread[0:1, :] * 64.0 + spread[1:2, :]
    place = (
        (blk * ROWS + chan * SLOT).astype(F32)
        + iota((1, ROWS), 1).astype(F32)
        - 7.0 * spread[2:3, :]
    )
    live = place < limit
    amps = amps_ref[...]
    slots = (
        dot_tn(weights(phr_ref, phc_ref, sixj, 0, live).astype(BF), amps)
        + dot_tn(weights(phr_ref, phc_ref, sixj, 1, live).astype(BF), amps)
    ).astype(BF)
    for k in range(4):
        lo, hi = FWD[k], FWD[k + 1]
        n = hi - lo
        r = iota((NZ * n, 1), 0)
        zz = r >> (5 if n == 32 else 4)
        rho = lo + (r & (n - 1))
        q = div28(rho)
        col = (q - k) * ROWS + zz * U + (rho - q * U)
        if k < 3:
            sel = onehot_rows(col, 2 * ROWS)
            piece = dot(sel[:, :ROWS], slots[:, 128 * k : 128 * k + 128]) + dot(
                sel[:, ROWS:], slots[:, 128 * k + 128 : 128 * k + 256]
            )
        else:
            piece = dot(onehot_rows(col, ROWS), slots[:, 128 * k : 128 * k + 128])
        sf[:, lo:hi, :] = piece.astype(BF).reshape(NZ, n, 128)

    pl.semaphore_wait(barrier, 31)

    def send_z(source, dest, lo, hi, send, recv):
        span = pl.ds(lo, hi - lo)

        def go(i, _):
            tz = z_target(i)
            pltpu.make_async_remote_copy(
                src_ref=source.at[tz, span],
                dst_ref=dest.at[z, span],
                send_sem=send,
                recv_sem=recv,
                device_id=(tz * NY + y, blk),
                device_id_type=MESH,
            ).start()
            return 0

        lax.fori_loop(0, 15, go, 0)
        pltpu.make_async_copy(source.at[z, span], dest.at[z, span], recv).start()

    def arrived(ref, sem):
        pltpu.make_async_copy(ref, ref, sem).wait()

    for k in range(4):
        send_z(sf, rf, FWD[k], FWD[k + 1], fs, fr.at[k])

    mixed = (
        weights(ppr_ref, ppc_ref, sixj, 0, None) + weights(ppr_ref, ppc_ref, sixj, 1, None)
    ).astype(BF)
    order = jnp.where(
        iota((ROWS, ROWS), 0) == natural_of(iota((1, ROWS), 1)), 1.0, 0.0
    ).astype(BF)
    mixed = dot(mixed, order).astype(BF)
    p2 = iota((1, 2 * ROWS), 1)
    half = jnp.where(p2 >= ROWS, ROWS, 0)
    order2 = jnp.where(
        iota((2 * ROWS, 2 * ROWS), 0) == half + natural_of(p2 - half), 1.0, 0.0
    ).astype(BF)
    load_inter.wait()
    for i in range(NX):
        cols = pl.ds(2 * ROWS * i, 2 * ROWS)
        part = dot_tn(mixed, inter[:, cols]).astype(BF)
        ip[:, cols] = dot(part, order2).astype(BF)

    p = iota((ROWS, 1), 0)
    py = div112(p)
    pr = p - py * 112
    pz = div7(pr)
    pu = py * SLOT + pr - pz * SLOT
    nz = div28(p)
    nu = p - nz * U
    for q in range(4):
        w0, w1 = WIN[q]
        win = w1 - w0
        off = U * q - w0
        mid[q][...] = onehot_rows(pz * win + off + pu, NZ * win)
        fin[q][...] = onehot_rows(nz * win + off + nu, NZ * win)
    for k in range(4):
        lo, hi = BWD[k], BWD[k + 1]
        n = hi - lo
        r = iota((NZ * n, 1), 0)
        zz = r >> (5 if n == 32 else 4)
        rho = lo + (r & (n - 1))
        q = div28(rho)
        u = rho - q * U
        uy = div7(u)
        first = max(k - 1, 0)
        col = (q - first) * ROWS + uy * 112 + zz * SLOT + (u - uy * SLOT)
        backs[k][...] = onehot_rows(col, ROWS if k == 0 else 2 * ROWS)
    diag = iota((ROWS, ROWS), 0) == iota((ROWS, ROWS), 1)
    pcol[...] = jnp.broadcast_to(
        jnp.sum(jnp.where(diag, pe_ref[...], 0.0), axis=1, keepdims=True), (ROWS, 128)
    )
    load_src.wait()

    def stage_yx(q):
        w0, w1 = WIN[q]
        arrived(rf.at[:, pl.ds(FWD[q], FWD[q + 1] - FWD[q])], fr.at[q])
        rows = rf[:, w0:w1, :].reshape(NZ * (w1 - w0), 128)
        sy[q] = dot(mid[q][...], rows).astype(BF).reshape(NY, 112, 128)

        def go(i, _):
            ty, tx = yx_target(i)
            pltpu.make_async_remote_copy(
                src_ref=sy.at[q, ty],
                dst_ref=g.at[q, x, core, y],
                send_sem=gs.at[q],
                recv_sem=gr.at[q],
                device_id=(z * NY + ty, tx * 2 + core),
                device_id_type=MESH,
            ).start()
            return 0

        lax.fori_loop(1, 16, go, 0)
        pltpu.make_async_copy(sy.at[q, y], g.at[q, x, core, y], gr.at[q]).start()

    def to_other(q):
        return pltpu.make_async_remote_copy(
            src_ref=g.at[q, :, core],
            dst_ref=g.at[q, :, core],
            send_sem=cs.at[q],
            recv_sem=cr.at[q],
            device_id=(chan, x * 2 + other),
            device_id_type=MESH,
        )

    def stage_core(q):
        arrived(g.at[q, :, core], gr.at[q])
        to_other(q).start()

    def stage_mul(q):
        arrived(g.at[q, :, other], cr.at[q])
        total = dot(ip[...], g[q].reshape(8 * ROWS, 128))
        ts[q] = total.astype(BF).reshape(NY, 112, 128)

        def go(i, _):
            ty = lax.rem(y + i, NY)
            pltpu.make_async_remote_copy(
                src_ref=ts.at[q, ty],
                dst_ref=ry.at[q, y],
                send_sem=ys.at[q],
                recv_sem=yr.at[q],
                device_id=(z * NY + ty, blk),
                device_id_type=MESH,
            ).start()
            return 0

        lax.fori_loop(1, 4, go, 0)
        pltpu.make_async_copy(ts.at[q, y], ry.at[q, y], yr.at[q]).start()

    def stage_back(k):
        lo, hi = BWD[k], BWD[k + 1]
        arrived(ry.at[k], yr.at[k])
        if k == 0:
            piece = dot(backs[k][...], ry[k].reshape(ROWS, 128))
        else:
            piece = dot(backs[k][...], ry[k - 1 : k + 1].reshape(2 * ROWS, 128))
        sb[:, lo:hi, :] = piece.astype(BF).reshape(NZ, hi - lo, 128)
        send_z(sb, rb, lo, hi, bs, br.at[k])

    limit_pp = pps_ref[chan]
    keep = blk * ROWS + iota((ROWS, 128), 0) < limit_pp

    def finish(q):
        w0, w1 = WIN[q]
        cols = slice(128 * q, 128 * q + 128)
        back = dot(fin[q][...], rb[:, w0:w1, :].reshape(NZ * (w1 - w0), 128))
        value = (src[:, cols].astype(F32) + back) / (pcol[...] - he_ref[:, cols])
        out_ref[:, cols] = jnp.where(keep, value, 0.0).astype(BF)

    def back_in(k):
        arrived(rb.at[:, pl.ds(BWD[k], BWD[k + 1] - BWD[k])], br.at[k])

    stage_yx(0)
    stage_yx(1)
    stage_core(0)
    stage_mul(0)
    stage_yx(2)
    stage_core(1)
    stage_back(0)
    stage_mul(1)
    stage_yx(3)
    stage_core(2)
    stage_back(1)
    stage_mul(2)
    stage_core(3)
    stage_back(2)
    stage_mul(3)
    stage_back(3)
    back_in(0)
    back_in(1)
    finish(0)
    back_in(2)
    finish(1)
    back_in(3)
    finish(2)
    finish(3)

    most = sf.at[pl.ds(0, 15)]
    arrived(most, fs)
    arrived(most, bs)
    for q in range(4):
        arrived(most, gs.at[q])
        arrived(g.at[q, :, core], cs.at[q])
        arrived(sf.at[pl.ds(0, 3)], ys.at[q])


def on_device(
    amps_pp,
    source_pp,
    cycle_interaction,
    to_ph_rows,
    to_ph_coef,
    to_pp_rows,
    to_pp_coef,
    sixj,
    pp_sizes,
    ph_sizes,
    particle_energy,
    hole_energy,
):
    vmem = pl.BlockSpec(memory_space=pltpu.VMEM)
    anywhere = pl.BlockSpec(memory_space=pl.ANY)
    smem = pl.BlockSpec(memory_space=pltpu.SMEM)
    wins = [NZ * (b - a) for a, b in WIN]
    cuts = [NZ * (b - a) for a, b in zip(BWD[:-1], BWD[1:])]
    dma = pltpu.SemaphoreType.DMA
    out = pl.pallas_call(
        kernel,
        out_shape=jax.ShapeDtypeStruct((ROWS, 512), BF),
        in_specs=[vmem] * 6 + [smem] + [vmem] * 3 + [anywhere] * 2,
        out_specs=vmem,
        scratch_shapes=[
            pltpu.VMEM((ROWS, 8 * ROWS), BF),
            pltpu.VMEM((ROWS, 512), BF),
            pltpu.VMEM((ROWS, 8 * ROWS), BF),
            pltpu.VMEM((NZ, STACK, 128), BF),
            pltpu.VMEM((NZ, STACK, 128), BF),
            pltpu.VMEM((4, NY, 112, 128), BF),
            pltpu.VMEM((4, NX, 2, NY, 112, 128), BF),
            pltpu.VMEM((4, NY, 112, 128), BF),
            pltpu.VMEM((4, NY, 112, 128), BF),
            pltpu.VMEM((NZ, STACK, 128), BF),
            pltpu.VMEM((NZ, STACK, 128), BF),
            *[pltpu.VMEM((ROWS, w), BF) for w in wins],
            *[pltpu.VMEM((c, ROWS if i == 0 else 2 * ROWS), BF) for i, c in enumerate(cuts)],
            *[pltpu.VMEM((ROWS, w), BF) for w in wins],
            pltpu.VMEM((ROWS, 128), F32),
            dma((2,)),
            dma,
            dma((4,)),
            dma((4,)),
            dma((4,)),
            dma((4,)),
            dma((4,)),
            dma((4,)),
            dma((4,)),
            dma,
            dma((4,)),
        ],
        compiler_params=pltpu.CompilerParams(
            collective_id=0, has_side_effects=True, vmem_limit_bytes=48 << 20
        ),
        name="cycle",
    )(
        amps_pp[0],
        to_ph_rows[0].T,
        to_ph_coef[0].T,
        to_pp_rows[0].T,
        to_pp_coef[0].T,
        sixj.reshape(1, 256),
        pp_sizes,
        ph_sizes.reshape(1, 64),
        particle_energy,
        hole_energy,
        cycle_interaction[0],
        source_pp[0],
    )
    return out[None]


def solution(mesh):
    in_specs = (
        P("chan", "blk", None),
        P("chan", "blk", None),
        P("chan", "blk", None),
        P("chan", "blk", None),
        P("chan", "blk", None),
        P("chan", "blk", None),
        P("chan", "blk", None),
        P(),
        P(),
        P(),
        P("chan", "blk"),
        P("chan", None),
    )
    out_specs = P("chan", "blk", None)
    return jax.shard_map(
        on_device, mesh=mesh, in_specs=in_specs, out_specs=out_specs, check_vma=False
    )
```

```python
import functools
import types

import jax
import jax.numpy as jnp
import ml_dtypes
import numpy as np
from jax import lax
from jax.experimental import pallas as pl
from jax.experimental.pallas import tpu as pltpu
from jax.sharding import PartitionSpec as P

MESH = pl.DeviceIdType.MESH
BF = jnp.bfloat16
F32 = jnp.float32
I32 = jnp.int32
NZ, NY, NX = 16, 4, 4
SLOT = 7
U = NY * SLOT
ROWS = NZ * U
STACK = 4 * U
FWD = (0, 32, 64, 96, 112)
BWD = (0, 16, 48, 80, 112)
WIN = ((0, 32), (16, 64), (48, 96), (80, 112))


def iota(shape, dim):
    return lax.broadcasted_iota(I32, shape, dim)


def natural_of(p):
    y, rest = p // 112, p % 112
    return (rest // SLOT * NY + y) * SLOT + rest % SLOT


def ones_at(columns, width):
    return jnp.asarray((np.arange(width)[None, :] == columns[:, None]).astype(ml_dtypes.bfloat16))


@functools.cache
def shapes():
    return {name: (len(columns), width) for name, (columns, width) in columns_of().items()}


def columns_of():
    p = np.arange(ROWS)
    found = {
        "order": (np.argsort(natural_of(p)), ROWS),
        "order2": (np.concatenate([np.argsort(natural_of(p)) + h * ROWS for h in range(2)]), 2 * ROWS),
    }
    z, u = p // U, p % U
    moved = natural_of(p)
    for q, (w0, w1) in enumerate(WIN):
        column = z * (w1 - w0) + U * q - w0 + u
        found[f"mid{q}"] = (column[moved], NZ * (w1 - w0))
        found[f"fin{q}"] = (column, NZ * (w1 - w0))
    for k in range(4):
        for name, cuts, first in (("pack", FWD, k), ("back", BWD, max(k - 1, 0))):
            lo, hi = cuts[k], cuts[k + 1]
            i = np.arange(NZ * (hi - lo))
            zz, rho = i // (hi - lo), lo + i % (hi - lo)
            q, u = rho // U, rho % U
            row = zz * U + u if name == "pack" else u // SLOT * 112 + zz * SLOT + u % SLOT
            wide = hi - lo == 32
            found[f"{name}{k}"] = ((q - first) * ROWS + row, ROWS * (2 if wide else 1))
    return found


def selections():
    return {name: ones_at(*value) for name, value in columns_of().items()}


def dot(a, b):
    return jnp.dot(a, b, preferred_element_type=F32)


def dot_tn(a, b):
    return lax.dot_general(a, b, (((0,), (0,)), ((), ())), preferred_element_type=F32)


def weights(rows_ref, coef_ref, sixj, k, live):
    c = 0.0
    for h in range(2):
        hit = iota((128, ROWS), 0) + 128 * h == coef_ref[k : k + 1, :]
        c = c + dot(sixj[h], jnp.where(hit, 1.0, 0.0).astype(BF))[0:1, :]
    if live is not None:
        c = jnp.where(live, c, 0.0)
    return jnp.where(iota((ROWS, ROWS), 0) == rows_ref[k : k + 1, :], c, 0.0)


INPUTS = ["amps", "phr", "phc", "ppr", "ppc", "sixj", "pps", "phs", "pe", "he", "inter", "src"]
STAGES = ["sf", "rf", "sy", "g", "ts", "ry", "sb", "rb", "scale", "out"]
SEMS = ["load", "store", "fs", "fr", "gs", "gr", "cs", "cr", "ys", "yr", "bs", "br"]


def kernel(*refs):
    tables = list(shapes())
    names = (
        [n + "_hbm" for n in INPUTS + tables]
        + ["out_hbm"]
        + INPUTS
        + tables
        + ["ip"]
        + STAGES
        + [n + "_sem" for n in SEMS]
    )
    body(types.SimpleNamespace(**dict(zip(names, refs, strict=True))))


def body(r):
    amps_ref, phr_ref, phc_ref, ppr_ref, ppc_ref = r.amps, r.phr, r.phc, r.ppr, r.ppc
    sixj_ref, pps_ref, phs_ref, pe_ref, he_ref = r.sixj, r.pps, r.phs, r.pe, r.he
    inter, src, ip, scale = r.inter, r.src, r.ip, r.scale
    sf, rf, sy, g, ts, ry, sb, rb = r.sf, r.rf, r.sy, r.g, r.ts, r.ry, r.sb, r.rb
    out_ref, out_hbm, store_sem = r.out, r.out_hbm, r.store_sem
    fs, fr, gs, gr, cs, cr = r.fs_sem, r.fr_sem, r.gs_sem, r.gr_sem, r.cs_sem, r.cr_sem
    ys, yr, bs, br = r.ys_sem, r.yr_sem, r.bs_sem, r.br_sem
    chan = lax.axis_index("chan")
    blk = lax.axis_index("blk")
    z = chan // NY
    y = lax.rem(chan, NY)
    x = blk // 2
    core = lax.rem(blk, 2)
    other = 1 - core

    def z_target(i):
        j = 15 - i - 1
        m = j // 2 + 1
        d = m + lax.rem(j, 2) * (NZ - 2 * m)
        return lax.rem(z + d, NZ)

    def yx_target(i):
        return lax.rem(y + lax.rem(i, NY), NY), lax.rem(x + i // NY, NX)

    queue = (
        "phr",
        "phc",
        "sixj",
        "phs",
        "amps",
        "pack0",
        "ppr",
        "ppc",
        "order",
        "inter",
        "order2",
        "pack1",
        "mid0",
        "mid1",
        "pack2",
        "pack3",
        "mid2",
        "mid3",
        "back0",
        "back1",
        "back2",
        "back3",
        "pps",
        "pe",
        "he",
        "src",
        "fin0",
        "fin1",
        "fin2",
        "fin3",
    )

    def load(name):
        k = queue.index(name)
        return pltpu.make_async_copy(
            getattr(r, name + "_hbm"), getattr(r, name), r.load_sem.at[k]
        )

    def loaded(*names):
        for name in names:
            load(name).wait()

    def table(name):
        loaded(name)
        return getattr(r, name)[...]

    barrier = pltpu.get_barrier_semaphore()

    def greet_z(i, _):
        pl.semaphore_signal(
            barrier, inc=1, device_id=(z_target(i) * NY + y, blk), device_id_type=MESH
        )
        return 0

    def greet_yx(i, _):
        ty, tx = yx_target(i)
        pl.semaphore_signal(
            barrier, inc=1, device_id=(z * NY + ty, tx * 2 + core), device_id_type=MESH
        )
        return 0

    lax.fori_loop(0, 15, greet_z, 0)
    lax.fori_loop(1, 16, greet_yx, 0)
    pl.semaphore_signal(barrier, inc=1, device_id=(chan, x * 2 + other), device_id_type=MESH)
    for name in queue[:6]:
        load(name).start()


    loaded("phr", "phc", "sixj", "phs", "amps")
    for name in queue[6:11]:
        load(name).start()
    six32 = sixj_ref[...].astype(F32)
    sixj = [jnp.broadcast_to(six32[h : h + 1, :], (16, 128)).astype(BF) for h in range(2)]
    s16 = iota((16, 64), 0)
    sizes = phs_ref[...]
    parts = jnp.where(
        s16 == 0,
        sizes >> 6,
        jnp.where(s16 == 1, sizes & 63, jnp.where(s16 == 2, iota((16, 64), 1), 0)),
    )
    offset = iota((64, ROWS), 1) - SLOT * iota((64, ROWS), 0)
    owner = (offset >= 0) & (offset < SLOT)
    spread = dot(parts.astype(F32).astype(BF), jnp.where(owner, 1.0, 0.0).astype(BF))
    limit = spread[0:1, :] * 64.0 + spread[1:2, :]
    place = (
        (blk * ROWS + chan * SLOT).astype(F32)
        + iota((1, ROWS), 1).astype(F32)
        - 7.0 * spread[2:3, :]
    )
    live = place < limit
    amps = amps_ref[...]
    slots = (
        dot_tn(weights(phr_ref, phc_ref, sixj, 0, live).astype(BF), amps)
        + dot_tn(weights(phr_ref, phc_ref, sixj, 1, live).astype(BF), amps)
    ).astype(BF)

    def pack(k):
        lo, hi = FWD[k], FWD[k + 1]
        sel = table(f"pack{k}")
        piece = dot(sel[:, :ROWS], slots[:, 128 * k : 128 * k + 128])
        if k < 3:
            piece = piece + dot(sel[:, ROWS:], slots[:, 128 * k + 128 : 128 * k + 256])
        sf[:, lo:hi, :] = piece.astype(BF).reshape(NZ, hi - lo, 128)

    pack(0)
    pl.semaphore_wait(barrier, 31)

    def send_z(source, dest, lo, hi, send, recv):
        span = pl.ds(lo, hi - lo)

        def go(i, _):
            tz = z_target(i)
            pltpu.make_async_remote_copy(
                src_ref=source.at[tz, span],
                dst_ref=dest.at[z, span],
                send_sem=send,
                recv_sem=recv,
                device_id=(tz * NY + y, blk),
                device_id_type=MESH,
            ).start()
            return 0

        lax.fori_loop(0, 15, go, 0)
        pltpu.make_async_copy(source.at[z, span], dest.at[z, span], recv).start()

    def arrived(ref, sem):
        pltpu.make_async_copy(ref, ref, sem).wait()

    def out_z(k):
        send_z(sf, rf, FWD[k], FWD[k + 1], fs.at[k], fr.at[k])

    def left_z(k):
        arrived(sf.at[pl.ds(0, 15), pl.ds(FWD[k], FWD[k + 1] - FWD[k])], fs.at[k])

    out_z(0)
    for name in queue[11:]:
        load(name).start()

    loaded("ppr", "ppc")
    mixed = (
        weights(ppr_ref, ppc_ref, sixj, 0, None) + weights(ppr_ref, ppc_ref, sixj, 1, None)
    ).astype(BF)
    mixed = dot(mixed, table("order")).astype(BF)
    loaded("inter", "order2")

    def mix(i):
        cols = pl.ds(2 * ROWS * i, 2 * ROWS)
        part = dot_tn(mixed, inter[:, cols]).astype(BF)
        ip[:, cols] = dot(part, r.order2[...]).astype(BF)

    def make_scale():
        loaded("pps", "pe", "he", "src")
        diag = iota((ROWS, ROWS), 0) == iota((ROWS, ROWS), 1)
        pcol = jnp.sum(jnp.where(diag, pe_ref[...], 0.0), axis=1, keepdims=True)
        keep = blk * ROWS + iota((ROWS, 512), 0) < pps_ref[0, chan]
        scale[...] = jnp.where(keep, 1.0 / (pcol - he_ref[...]), 0.0)

    def stage_yx(q):
        w0, w1 = WIN[q]
        arrived(rf.at[:, pl.ds(FWD[q], FWD[q + 1] - FWD[q])], fr.at[q])
        rows = rf[:, w0:w1, :].reshape(NZ * (w1 - w0), 128)
        sy[q] = dot(table(f"mid{q}"), rows).astype(BF).reshape(NY, 112, 128)

        def go(i, _):
            ty, tx = yx_target(i)
            pltpu.make_async_remote_copy(
                src_ref=sy.at[q, ty],
                dst_ref=g.at[q, x, core, y],
                send_sem=gs.at[q],
                recv_sem=gr.at[q, x],
                device_id=(z * NY + ty, tx * 2 + core),
                device_id_type=MESH,
            ).start()
            return 0

        lax.fori_loop(1, 16, go, 0)
        pltpu.make_async_copy(sy.at[q, y], g.at[q, x, core, y], gr.at[q, x]).start()

    chips = [lax.rem(x + d, NX) for d in (0, 1, 3, 2)]

    def stage_core(q):
        for xs in chips:
            arrived(g.at[q, xs, core], gr.at[q, xs])
            pltpu.make_async_remote_copy(
                src_ref=g.at[q, xs, core],
                dst_ref=g.at[q, xs, core],
                send_sem=cs.at[q],
                recv_sem=cr.at[q, xs],
                device_id=(chan, x * 2 + other),
                device_id_type=MESH,
            ).start()

    def stage_mul(q):
        total = jnp.zeros((ROWS, 128), F32)
        for xs in chips:
            arrived(g.at[q, xs, other], cr.at[q, xs])
            cols = pl.ds(pl.multiple_of(xs * 2 * ROWS, 128), 2 * ROWS)
            total = total + dot(ip[:, cols], g[q, xs].reshape(2 * ROWS, 128))
        ts[q] = total.astype(BF).reshape(NY, 112, 128)

        def go(i, _):
            ty = lax.rem(y + i, NY)
            pltpu.make_async_remote_copy(
                src_ref=ts.at[q, ty],
                dst_ref=ry.at[q, y],
                send_sem=ys.at[q],
                recv_sem=yr.at[q],
                device_id=(z * NY + ty, blk),
                device_id_type=MESH,
            ).start()
            return 0

        lax.fori_loop(1, 4, go, 0)
        pltpu.make_async_copy(ts.at[q, y], ry.at[q, y], yr.at[q]).start()

    def stage_back(k):
        lo, hi = BWD[k], BWD[k + 1]
        arrived(ry.at[k], yr.at[k])
        sel = table(f"back{k}")
        if k == 0:
            piece = dot(sel, ry[k].reshape(ROWS, 128))
        else:
            piece = dot(sel, ry[k - 1 : k + 1].reshape(2 * ROWS, 128))
        sb[:, lo:hi, :] = piece.astype(BF).reshape(NZ, hi - lo, 128)
        send_z(sb, rb, lo, hi, bs, br.at[k])

    def store(q):
        cols = pl.ds(128 * q, 128)
        return pltpu.make_async_copy(
            out_ref.at[:, cols], out_hbm.at[:, cols], store_sem.at[q]
        )

    def finish(q):
        w0, w1 = WIN[q]
        cols = slice(128 * q, 128 * q + 128)
        back = dot(table(f"fin{q}"), rb[:, w0:w1, :].reshape(NZ * (w1 - w0), 128))
        value = (src[:, cols].astype(F32) + back) * scale[:, cols]
        out_ref[:, cols] = value.astype(BF)
        store(q).start()

    def back_in(k):
        arrived(rb.at[:, pl.ds(BWD[k], BWD[k + 1] - BWD[k])], br.at[k])

    mix(0)
    pack(1)
    mix(1)
    mix(2)
    left_z(0)
    out_z(1)
    pack(2)
    pack(3)
    stage_yx(0)
    mix(3)
    left_z(1)
    out_z(2)
    stage_yx(1)
    stage_core(0)
    stage_mul(0)
    left_z(2)
    out_z(3)
    stage_yx(2)
    stage_core(1)
    stage_back(0)
    stage_mul(1)
    stage_yx(3)
    stage_core(2)
    stage_back(1)
    stage_mul(2)
    stage_core(3)
    stage_back(2)
    stage_mul(3)
    make_scale()
    stage_back(3)
    back_in(0)
    back_in(1)
    finish(0)
    back_in(2)
    finish(1)
    back_in(3)
    finish(2)
    finish(3)
    for q in range(4):
        store(q).wait()
    most = sf.at[pl.ds(0, 15)]
    left_z(3)
    arrived(most, bs)
    for q in range(4):
        arrived(most, gs.at[q])
        arrived(g.at[q, :, core], cs.at[q])
        arrived(sf.at[pl.ds(0, 3)], ys.at[q])


def on_device(
    amps_pp,
    source_pp,
    cycle_interaction,
    to_ph_rows,
    to_ph_coef,
    to_pp_rows,
    to_pp_coef,
    sixj,
    pp_sizes,
    ph_sizes,
    particle_energy,
    hole_energy,
):
    hbm = pl.BlockSpec(memory_space=pltpu.HBM)
    dma = pltpu.SemaphoreType.DMA
    tables = selections()
    inputs = (
        amps_pp[0],
        to_ph_rows[0].T,
        to_ph_coef[0].T,
        to_pp_rows[0].T,
        to_pp_coef[0].T,
        sixj.reshape(2, 128),
        pp_sizes.reshape(1, 64),
        ph_sizes.reshape(1, 64),
        particle_energy,
        hole_energy,
        cycle_interaction[0],
        source_pp[0],
        *tables.values(),
    )
    held = [
        (pltpu.SMEM if name == "pps" else pltpu.VMEM)(value.shape, value.dtype)
        for name, value in zip(INPUTS + list(tables), inputs, strict=True)
    ]
    out = pl.pallas_call(
        kernel,
        out_shape=jax.ShapeDtypeStruct((ROWS, 512), BF),
        in_specs=[hbm] * len(inputs),
        out_specs=hbm,
        scratch_shapes=[
            *held,
            pltpu.VMEM((ROWS, 8 * ROWS), BF),
            pltpu.VMEM((NZ, STACK, 128), BF),
            pltpu.VMEM((NZ, STACK, 128), BF),
            pltpu.VMEM((4, NY, 112, 128), BF),
            pltpu.VMEM((4, NX, 2, NY, 112, 128), BF),
            pltpu.VMEM((4, NY, 112, 128), BF),
            pltpu.VMEM((4, NY, 112, 128), BF),
            pltpu.VMEM((NZ, STACK, 128), BF),
            pltpu.VMEM((NZ, STACK, 128), BF),
            pltpu.VMEM((ROWS, 512), F32),
            pltpu.VMEM((ROWS, 512), BF),
            dma((len(inputs),)),
            dma((4,)),
            dma((4,)),
            dma((4,)),
            dma((4,)),
            dma((4, NX)),
            dma((4,)),
            dma((4, NX)),
            dma((4,)),
            dma((4,)),
            dma,
            dma((4,)),
        ],
        compiler_params=pltpu.CompilerParams(
            collective_id=0, has_side_effects=True, vmem_limit_bytes=60 << 20
        ),
        name="cycle",
    )(*inputs)
    return out[None]


def solution(mesh):
    in_specs = (
        P("chan", "blk", None),
        P("chan", "blk", None),
        P("chan", "blk", None),
        P("chan", "blk", None),
        P("chan", "blk", None),
        P("chan", "blk", None),
        P("chan", "blk", None),
        P(),
        P(),
        P(),
        P("chan", "blk"),
        P("chan", None),
    )
    out_specs = P("chan", "blk", None)
    return jax.shard_map(
        on_device, mesh=mesh, in_specs=in_specs, out_specs=out_specs, check_vma=False
    )
```

```python
import functools
import types

import jax
import jax.numpy as jnp
import ml_dtypes
import numpy as np
from jax import lax
from jax.experimental import pallas as pl
from jax.experimental.pallas import tpu as pltpu
from jax.sharding import PartitionSpec as P

MESH = pl.DeviceIdType.MESH
BF = jnp.bfloat16
F32 = jnp.float32
I32 = jnp.int32
NZ, NY, NX = 16, 4, 4
SLOT = 7
U = NY * SLOT
ROWS = NZ * U
STACK = 4 * U
FWD = (0, 32, 64, 96, 112)
BWD = (0, 16, 48, 80, 112)
WIN = ((0, 32), (16, 64), (48, 96), (80, 112))


def iota(shape, dim):
    return lax.broadcasted_iota(I32, shape, dim)


def natural_of(p):
    y, rest = p // 112, p % 112
    return (rest // SLOT * NY + y) * SLOT + rest % SLOT


def ones_at(columns, width):
    return jnp.asarray((np.arange(width)[None, :] == columns[:, None]).astype(ml_dtypes.bfloat16))


@functools.cache
def shapes():
    return {name: (len(columns), width) for name, (columns, width) in columns_of().items()}


def columns_of():
    p = np.arange(ROWS)
    found = {
        "order": (np.argsort(natural_of(p)), ROWS),
        "order2": (np.concatenate([np.argsort(natural_of(p)) + h * ROWS for h in range(2)]), 2 * ROWS),
    }
    z, u = p // U, p % U
    moved = natural_of(p)
    for q, (w0, w1) in enumerate(WIN):
        column = z * (w1 - w0) + U * q - w0 + u
        found[f"mid{q}"] = (column[moved], NZ * (w1 - w0))
        found[f"fin{q}"] = (column, NZ * (w1 - w0))
    for k in range(4):
        for name, cuts, first in (("pack", FWD, k), ("back", BWD, max(k - 1, 0))):
            lo, hi = cuts[k], cuts[k + 1]
            i = np.arange(NZ * (hi - lo))
            zz, rho = i // (hi - lo), lo + i % (hi - lo)
            q, u = rho // U, rho % U
            row = zz * U + u if name == "pack" else u // SLOT * 112 + zz * SLOT + u % SLOT
            wide = hi - lo == 32
            found[f"{name}{k}"] = ((q - first) * ROWS + row, ROWS * (2 if wide else 1))
    return found


def selections():
    return {name: ones_at(*value) for name, value in columns_of().items()}


def dot(a, b):
    return jnp.dot(a, b, preferred_element_type=F32)


def dot_tn(a, b):
    return lax.dot_general(a, b, (((0,), (0,)), ((), ())), preferred_element_type=F32)


def weights(rows_ref, coef_ref, sixj, k, live):
    c = 0.0
    for h in range(2):
        hit = iota((128, ROWS), 0) + 128 * h == coef_ref[k : k + 1, :]
        c = c + dot(sixj[h], jnp.where(hit, 1.0, 0.0).astype(BF))[0:1, :]
    if live is not None:
        c = jnp.where(live, c, 0.0)
    return jnp.where(iota((ROWS, ROWS), 0) == rows_ref[k : k + 1, :], c, 0.0)


INPUTS = ["amps", "phr", "phc", "ppr", "ppc", "sixj", "pps", "phs", "pe", "he", "inter", "src"]
STAGES = ["sf", "rf", "sy", "g", "ts", "ry", "sb", "rb", "scale", "out"]
SEMS = ["load", "store", "fs", "fr", "gs", "gr", "cs", "cr", "ys", "yr", "bs", "br"]


def kernel(*refs):
    tables = list(shapes())
    names = (
        [n + "_hbm" for n in INPUTS + tables]
        + ["out_hbm"]
        + INPUTS
        + tables
        + ["ip"]
        + STAGES
        + [n + "_sem" for n in SEMS]
    )
    body(types.SimpleNamespace(**dict(zip(names, refs, strict=True))))


def body(r):
    amps_ref, phr_ref, phc_ref, ppr_ref, ppc_ref = r.amps, r.phr, r.phc, r.ppr, r.ppc
    sixj_ref, pps_ref, phs_ref, pe_ref, he_ref = r.sixj, r.pps, r.phs, r.pe, r.he
    inter, src, ip, scale = r.inter, r.src, r.ip, r.scale
    sf, rf, sy, g, ts, ry, sb, rb = r.sf, r.rf, r.sy, r.g, r.ts, r.ry, r.sb, r.rb
    out_ref, out_hbm, store_sem = r.out, r.out_hbm, r.store_sem
    fs, fr, gs, gr, cs, cr = r.fs_sem, r.fr_sem, r.gs_sem, r.gr_sem, r.cs_sem, r.cr_sem
    ys, yr, bs, br = r.ys_sem, r.yr_sem, r.bs_sem, r.br_sem
    chan = lax.axis_index("chan")
    blk = lax.axis_index("blk")
    z = chan // NY
    y = lax.rem(chan, NY)
    x = blk // 2
    core = lax.rem(blk, 2)
    other = 1 - core

    def z_target(i):
        j = 15 - i - 1
        m = j // 2 + 1
        d = m + lax.rem(j, 2) * (NZ - 2 * m)
        return lax.rem(z + d, NZ)

    def yx_target(i):
        return lax.rem(y + lax.rem(i, NY), NY), lax.rem(x + i // NY, NX)

    queue = (
        "phr",
        "phc",
        "sixj",
        "phs",
        "amps",
        "pack0",
        "ppr",
        "ppc",
        "order",
        "inter",
        "order2",
        "pack1",
        "mid0",
        "mid1",
        "pack2",
        "pack3",
        "mid2",
        "mid3",
        "back0",
        "back1",
        "back2",
        "back3",
        "pps",
        "pe",
        "he",
        "src",
        "fin0",
        "fin1",
        "fin2",
        "fin3",
    )

    def load(name):
        k = queue.index(name)
        return pltpu.make_async_copy(
            getattr(r, name + "_hbm"), getattr(r, name), r.load_sem.at[k]
        )

    def loaded(*names):
        for name in names:
            load(name).wait()

    def table(name):
        loaded(name)
        return getattr(r, name)[...]

    barrier = pltpu.get_barrier_semaphore()

    def greet_z(i, _):
        pl.semaphore_signal(
            barrier, inc=1, device_id=(z_target(i) * NY + y, blk), device_id_type=MESH
        )
        return 0

    def greet_yx(i, _):
        ty, tx = yx_target(i)
        pl.semaphore_signal(
            barrier, inc=1, device_id=(z * NY + ty, tx * 2 + core), device_id_type=MESH
        )
        return 0

    lax.fori_loop(0, 15, greet_z, 0)
    lax.fori_loop(1, 16, greet_yx, 0)
    pl.semaphore_signal(barrier, inc=1, device_id=(chan, x * 2 + other), device_id_type=MESH)
    for name in queue[:6]:
        load(name).start()


    loaded("phr", "phc", "sixj", "phs", "amps")
    for name in queue[6:11]:
        load(name).start()
    six32 = sixj_ref[...].astype(F32)
    sixj = [jnp.broadcast_to(six32[h : h + 1, :], (16, 128)).astype(BF) for h in range(2)]
    s16 = iota((16, 64), 0)
    sizes = phs_ref[...]
    parts = jnp.where(
        s16 == 0,
        sizes >> 6,
        jnp.where(s16 == 1, sizes & 63, jnp.where(s16 == 2, iota((16, 64), 1), 0)),
    )
    offset = iota((64, ROWS), 1) - SLOT * iota((64, ROWS), 0)
    owner = (offset >= 0) & (offset < SLOT)
    spread = dot(parts.astype(F32).astype(BF), jnp.where(owner, 1.0, 0.0).astype(BF))
    limit = spread[0:1, :] * 64.0 + spread[1:2, :]
    place = (
        (blk * ROWS + chan * SLOT).astype(F32)
        + iota((1, ROWS), 1).astype(F32)
        - 7.0 * spread[2:3, :]
    )
    live = place < limit
    amps = amps_ref[...]
    slots = (
        dot_tn(weights(phr_ref, phc_ref, sixj, 0, live).astype(BF), amps)
        + dot_tn(weights(phr_ref, phc_ref, sixj, 1, live).astype(BF), amps)
    ).astype(BF)

    def pack(k):
        lo, hi = FWD[k], FWD[k + 1]
        sel = table(f"pack{k}")
        piece = dot(sel[:, :ROWS], slots[:, 128 * k : 128 * k + 128])
        if k < 3:
            piece = piece + dot(sel[:, ROWS:], slots[:, 128 * k + 128 : 128 * k + 256])
        sf[:, lo:hi, :] = piece.astype(BF).reshape(NZ, hi - lo, 128)

    pack(0)
    pl.semaphore_wait(barrier, 31)

    def send_z(source, dest, lo, hi, send, recv):
        span = pl.ds(lo, hi - lo)

        def go(i, _):
            tz = z_target(i)
            pltpu.make_async_remote_copy(
                src_ref=source.at[tz, span],
                dst_ref=dest.at[z, span],
                send_sem=send,
                recv_sem=recv,
                device_id=(tz * NY + y, blk),
                device_id_type=MESH,
            ).start()
            return 0

        lax.fori_loop(0, 15, go, 0)
        pltpu.make_async_copy(source.at[z, span], dest.at[z, span], recv).start()

    def arrived(ref, sem):
        pltpu.make_async_copy(ref, ref, sem).wait()

    def out_z(k):
        send_z(sf, rf, FWD[k], FWD[k + 1], fs.at[k], fr.at[k])

    def left_z(k):
        arrived(sf.at[pl.ds(0, 15), pl.ds(FWD[k], FWD[k + 1] - FWD[k])], fs.at[k])

    out_z(0)
    for name in queue[11:]:
        load(name).start()

    loaded("ppr", "ppc")
    mixed = (
        weights(ppr_ref, ppc_ref, sixj, 0, None) + weights(ppr_ref, ppc_ref, sixj, 1, None)
    ).astype(BF)
    mixed = dot(mixed, table("order")).astype(BF)
    loaded("inter", "order2")

    def mix(i):
        cols = pl.ds(2 * ROWS * i, 2 * ROWS)
        part = dot_tn(mixed, inter[:, cols]).astype(BF)
        ip[:, cols] = dot(part, r.order2[...]).astype(BF)

    def make_scale():
        loaded("pps", "pe", "he", "src")
        diag = iota((ROWS, ROWS), 0) == iota((ROWS, ROWS), 1)
        pcol = jnp.sum(jnp.where(diag, pe_ref[...], 0.0), axis=1, keepdims=True)
        keep = blk * ROWS + iota((ROWS, 512), 0) < pps_ref[0, chan]
        scale[...] = jnp.where(keep, 1.0 / (pcol - he_ref[...]), 0.0)

    def stage_yx(q):
        w0, w1 = WIN[q]
        arrived(rf.at[:, pl.ds(FWD[q], FWD[q + 1] - FWD[q])], fr.at[q])
        rows = rf[:, w0:w1, :].reshape(NZ * (w1 - w0), 128)
        sy[q] = dot(table(f"mid{q}"), rows).astype(BF).reshape(NY, 112, 128)

        def go(i, _):
            ty, tx = yx_target(i)
            pltpu.make_async_remote_copy(
                src_ref=sy.at[q, ty],
                dst_ref=g.at[q, x, core, y],
                send_sem=gs.at[q],
                recv_sem=gr.at[q, x],
                device_id=(z * NY + ty, tx * 2 + core),
                device_id_type=MESH,
            ).start()
            return 0

        for dx in (2, 1, 3, 0):
            lax.fori_loop(4 * dx + (dx == 0), 4 * dx + 4, go, 0)
        pltpu.make_async_copy(sy.at[q, y], g.at[q, x, core, y], gr.at[q, x]).start()

    chips = [lax.rem(x + d, NX) for d in (0, 1, 3, 2)]

    def stage_core(q):
        for xs in chips:
            arrived(g.at[q, xs, core], gr.at[q, xs])
            pltpu.make_async_remote_copy(
                src_ref=g.at[q, xs, core],
                dst_ref=g.at[q, xs, core],
                send_sem=cs.at[q],
                recv_sem=cr.at[q, xs],
                device_id=(chan, x * 2 + other),
                device_id_type=MESH,
            ).start()

    def stage_mul(q):
        total = jnp.zeros((ROWS, 128), F32)
        for xs in chips:
            arrived(g.at[q, xs, other], cr.at[q, xs])
            cols = pl.ds(pl.multiple_of(xs * 2 * ROWS, 128), 2 * ROWS)
            total = total + dot(ip[:, cols], g[q, xs].reshape(2 * ROWS, 128))
        ts[q] = total.astype(BF).reshape(NY, 112, 128)

        def go(i, _):
            ty = lax.rem(y + lax.rem(i, 3) + 1, NY)
            pltpu.make_async_remote_copy(
                src_ref=ts.at[q, ty],
                dst_ref=ry.at[q, y],
                send_sem=ys.at[q],
                recv_sem=yr.at[q],
                device_id=(z * NY + ty, blk),
                device_id_type=MESH,
            ).start()
            return 0

        lax.fori_loop(1, 4, go, 0)
        pltpu.make_async_copy(ts.at[q, y], ry.at[q, y], yr.at[q]).start()

    def stage_back(k):
        lo, hi = BWD[k], BWD[k + 1]
        arrived(ry.at[k], yr.at[k])
        sel = table(f"back{k}")
        if k == 0:
            piece = dot(sel, ry[k].reshape(ROWS, 128))
        else:
            piece = dot(sel, ry[k - 1 : k + 1].reshape(2 * ROWS, 128))
        sb[:, lo:hi, :] = piece.astype(BF).reshape(NZ, hi - lo, 128)
        send_z(sb, rb, lo, hi, bs, br.at[k])

    def store(q):
        cols = pl.ds(128 * q, 128)
        return pltpu.make_async_copy(
            out_ref.at[:, cols], out_hbm.at[:, cols], store_sem.at[q]
        )

    def finish(q):
        w0, w1 = WIN[q]
        cols = slice(128 * q, 128 * q + 128)
        back = dot(table(f"fin{q}"), rb[:, w0:w1, :].reshape(NZ * (w1 - w0), 128))
        value = (src[:, cols].astype(F32) + back) * scale[:, cols]
        out_ref[:, cols] = value.astype(BF)
        store(q).start()

    def back_in(k):
        arrived(rb.at[:, pl.ds(BWD[k], BWD[k + 1] - BWD[k])], br.at[k])

    mix(0)
    pack(1)
    mix(1)
    mix(2)
    left_z(0)
    out_z(1)
    pack(2)
    pack(3)
    stage_yx(0)
    mix(3)
    left_z(1)
    out_z(2)
    stage_yx(1)
    stage_core(0)
    stage_mul(0)
    left_z(2)
    out_z(3)
    stage_yx(2)
    stage_core(1)
    stage_back(0)
    stage_mul(1)
    stage_yx(3)
    stage_core(2)
    stage_back(1)
    stage_mul(2)
    stage_core(3)
    stage_back(2)
    stage_mul(3)
    make_scale()
    stage_back(3)
    back_in(0)
    back_in(1)
    finish(0)
    back_in(2)
    finish(1)
    back_in(3)
    finish(2)
    finish(3)
    for q in range(4):
        store(q).wait()
    most = sf.at[pl.ds(0, 15)]
    left_z(3)
    arrived(most, bs)
    for q in range(4):
        arrived(most, gs.at[q])
        arrived(g.at[q, :, core], cs.at[q])
        arrived(sf.at[pl.ds(0, 3)], ys.at[q])


def on_device(
    amps_pp,
    source_pp,
    cycle_interaction,
    to_ph_rows,
    to_ph_coef,
    to_pp_rows,
    to_pp_coef,
    sixj,
    pp_sizes,
    ph_sizes,
    particle_energy,
    hole_energy,
):
    hbm = pl.BlockSpec(memory_space=pltpu.HBM)
    dma = pltpu.SemaphoreType.DMA
    tables = selections()
    inputs = (
        amps_pp[0],
        to_ph_rows[0].T,
        to_ph_coef[0].T,
        to_pp_rows[0].T,
        to_pp_coef[0].T,
        sixj.reshape(2, 128),
        pp_sizes.reshape(1, 64),
        ph_sizes.reshape(1, 64),
        particle_energy,
        hole_energy,
        cycle_interaction[0],
        source_pp[0],
        *tables.values(),
    )
    held = [
        (pltpu.SMEM if name == "pps" else pltpu.VMEM)(value.shape, value.dtype)
        for name, value in zip(INPUTS + list(tables), inputs, strict=True)
    ]
    out = pl.pallas_call(
        kernel,
        out_shape=jax.ShapeDtypeStruct((ROWS, 512), BF),
        in_specs=[hbm] * len(inputs),
        out_specs=hbm,
        scratch_shapes=[
            *held,
            pltpu.VMEM((ROWS, 8 * ROWS), BF),
            pltpu.VMEM((NZ, STACK, 128), BF),
            pltpu.VMEM((NZ, STACK, 128), BF),
            pltpu.VMEM((4, NY, 112, 128), BF),
            pltpu.VMEM((4, NX, 2, NY, 112, 128), BF),
            pltpu.VMEM((4, NY, 112, 128), BF),
            pltpu.VMEM((4, NY, 112, 128), BF),
            pltpu.VMEM((NZ, STACK, 128), BF),
            pltpu.VMEM((NZ, STACK, 128), BF),
            pltpu.VMEM((ROWS, 512), F32),
            pltpu.VMEM((ROWS, 512), BF),
            dma((len(inputs),)),
            dma((4,)),
            dma((4,)),
            dma((4,)),
            dma((4,)),
            dma((4, NX)),
            dma((4,)),
            dma((4, NX)),
            dma((4,)),
            dma((4,)),
            dma,
            dma((4,)),
        ],
        compiler_params=pltpu.CompilerParams(
            collective_id=0, has_side_effects=True, vmem_limit_bytes=60 << 20
        ),
        name="cycle",
    )(*inputs)
    return out[None]


def solution(mesh):
    in_specs = (
        P("chan", "blk", None),
        P("chan", "blk", None),
        P("chan", "blk", None),
        P("chan", "blk", None),
        P("chan", "blk", None),
        P("chan", "blk", None),
        P("chan", "blk", None),
        P(),
        P(),
        P(),
        P("chan", "blk"),
        P("chan", None),
    )
    out_specs = P("chan", "blk", None)
    return jax.shard_map(
        on_device, mesh=mesh, in_specs=in_specs, out_specs=out_specs, check_vma=False
    )
```
